32 devices in a mesh: row: 8 (over y, x, core), col: 4 (over z).
Axes of the slice: x: 2, y: 2, z: 4, core: 2. Of those that a mesh axis runs over, the one named last changes fastest.
Arguments:
- activations: bfloat16 [768, 16384], P(('row', 'col')), may hold values from -14 to 14
- tenant_ids: int32 [768], P(('row', 'col')), may hold values from 0 to 63
- concept_labels: int32 [768], P(('row', 'col')), may hold values from 0 to 1
Outputs:
- covariance: float32 [16384, 16384], P('row', 'col')
- cross: float32 [128, 16384], P(None, ('row', 'col'))
The draws below stay inside these ranges and needn't reach their ends.
All inputs are finite; a program needn't handle non-finite values.
Results may differ from the reference program's by a relative error of at most 0.0003.
Values may be sent and summed in bfloat16 or wider, within the bound.
No kernel may reach another device: no remote copies, remote signals or barrier semaphores. Data moves between devices by JAX's collectives and lax.ppermute only.
A program may use at most 128 MiB of HBM per device.

```python
import math
import jax
import jax.numpy as jnp
import numpy as np

D = 16384
TENANTS = 64
LABELS = 2
TOKENS = 768


def draw_activations(key, part):
    base_key = jax.random.fold_in(key, 11)
    key_base, key_scale, key_offset = jax.random.split(base_key, 3)
    scales = jnp.exp(jax.random.uniform(key_scale, (D,), jnp.float32, jnp.log(0.4), jnp.log(2.0)))
    offset = jax.random.uniform(key_offset, (D,), jnp.float32, -1.0, 1.0)
    base = jax.random.normal(key_base, (TOKENS, D), jnp.float32)
    values = base * scales[None, :] + offset[None, :]
    values = jnp.clip(values, -14.0, 14.0)
    return values.astype(jnp.bfloat16)


def plant(array, stream_key, low, largest):
    longest = array.shape.index(max(array.shape))
    spots = []
    for shift in (0, 1):
        where = [jax.random.randint(jax.random.fold_in(stream_key, axis), (), 0, length) for axis, length in enumerate(array.shape)]
        where[longest] = (where[longest] + shift) % array.shape[longest]
        spots.append(tuple(where))
    return array.at[spots[0]].set(low).at[spots[1]].set(largest)


def rank_table(amount, slope):
    portions = [(1 << 20) // math.isqrt(grade ** slope) + 1 for grade in range(1, amount + 1)]
    spread = 1 + sum(portions) // (1 << 30)
    return np.cumsum(np.array([max(1, weight // spread) for weight in portions]))


def ranked_ids(stream_key, dims, amount, slope):
    grid = rank_table(amount, slope)
    ticket = jax.random.randint(jax.random.fold_in(stream_key, 1), dims, 0, int(grid[amount - 1]))
    standing = jnp.searchsorted(jnp.asarray(grid, jnp.int32), ticket, side="right")
    return jax.random.permutation(jax.random.fold_in(stream_key, 2), amount)[standing].astype(jnp.int32)


def setup_inputs(seed: int = 0) -> dict:
    key_list = jax.random.split(jax.random.key(seed), 4)
    return {
        "activations": draw_activations(jax.random.fold_in(key_list[3], 71), 0),
        "tenant_ids": plant(ranked_ids(key_list[1], (TOKENS,), TENANTS, 2), jax.random.fold_in(key_list[1], 3), 0, TENANTS - 1).astype(jnp.int32),
        "concept_labels": plant(jax.random.randint(key_list[2], (TOKENS,), 0, LABELS), jax.random.fold_in(key_list[2], 1), 0, LABELS - 1).astype(jnp.int32),
    }


def reference(activations, tenant_ids, concept_labels):
    total = activations.shape[0]
    mean = jnp.sum(activations, axis=0, dtype=jnp.float32) / total
    gram = jnp.dot(activations.T, activations, preferred_element_type=jnp.float32)
    covariance = gram / total - mean[:, None] * mean[None, :]
    groups = TENANTS * LABELS
    codes = tenant_ids * LABELS + concept_labels
    onehot = codes[:, None] == jnp.arange(groups, dtype=jnp.int32)[None, :]
    counts = jnp.sum(onehot.astype(jnp.float32), axis=0)
    sums = jnp.dot(onehot.astype(jnp.bfloat16).T, activations, preferred_element_type=jnp.float32)
    cross = (groups / total) * (sums - counts[:, None] * mean[None, :])
    return covariance, cross
```

```python
import functools

import jax
import jax.numpy as jnp
from jax import lax
from jax.experimental import pallas as pl
from jax.experimental.pallas import tpu as pltpu
from jax.sharding import PartitionSpec as P

TENANTS = 64
LABELS = 2
LANES = 128
MIB = 1024 * 1024

COST = pl.CostEstimate(flops=0, bytes_accessed=0, transcendentals=0)

ANY = pl.BlockSpec(memory_space=pl.ANY)
WHOLE = pl.BlockSpec(memory_space=pltpu.VMEM)
SCALARS = pl.BlockSpec(memory_space=pltpu.SMEM)


def params(mib):
    return pltpu.CompilerParams(vmem_limit_bytes=mib * MIB)


def swap_rows(x, mask):
    return lax.ppermute(x, "row", [(i, i ^ mask) for i in range(lax.axis_size("row"))])


def swap_cols(x, mask):
    return lax.ppermute(x, "col", [(i, i ^ mask) for i in range(lax.axis_size("col"))])


def pair_cols(x, first):
    pairs = []
    for low in range(first, lax.axis_size("col") - 1, 2):
        pairs += [(low, low + 1), (low + 1, low)]
    return lax.ppermute(x, "col", pairs)


def place():
    row = lax.axis_index("row")
    return row // 2, row % 2, lax.axis_index("col")


def deal_kernel(chips, tenants, labels, features, *outs):
    local, total = features.shape
    chip, _, col = place()
    row_outs, col_outs = outs[:chips], outs[chips:]
    width = total // len(col_outs)
    token = lax.broadcasted_iota(jnp.int32, (local, LANES), 0)
    codes = jnp.zeros((local, LANES), jnp.int32)
    for index in range(local):
        codes = jnp.where(token == index, tenants[index] * LABELS + labels[index], codes)
    codes = codes.astype(jnp.float32).astype(jnp.bfloat16)
    for mask, out in enumerate(col_outs):
        start = pl.multiple_of((col ^ mask) * width, LANES)
        out[:, :width] = features[:, pl.ds(start, width)]
        out[:, width:] = codes
    for mask, out in enumerate(row_outs):
        block = out.shape[1]
        start = pl.multiple_of((chip ^ mask) * block, LANES)
        out[...] = features[:, pl.ds(start, block)]


def share_kernel(*refs):
    *parts, out = refs
    _, core, _ = place()
    width = out.shape[2]
    start = pl.multiple_of((1 - core) * width, LANES)
    for index, part in enumerate(parts):
        out[index] = part[:, pl.ds(start, width)]


def rows_kernel(parts, *refs):
    shared = refs[parts]
    _, core, _ = place()
    rows = 2 * shared.shape[1]
    for index in range(parts):
        start = 0
        for out in refs[parts + 1 :]:
            width = out.shape[1]
            begin = pl.multiple_of(core * shared.shape[2] + start, LANES)
            both = jnp.concatenate([refs[index][:, pl.ds(begin, width)], shared[index, :, pl.ds(start, width)]], axis=0)
            out[index * rows : (index + 1) * rows, :] = both
            start += width


def stack_kernel(*refs):
    *parts, out = refs
    for index, part in enumerate(parts):
        out[index] = part[...]


def column_kernel(chips, *refs):
    near, far = refs[:chips], refs[chips : 2 * chips]
    panel, mean, member = refs[2 * chips :]
    total, columns = panel.shape
    planes, local, _ = near[0].shape
    step = min(512, columns)
    ones = jnp.ones((16, total), jnp.bfloat16)
    lanes = lax.broadcasted_iota(jnp.int32, (2 * local, LANES), 1).astype(jnp.float32)
    for start in range(0, columns, step):
        span = pl.ds(start, step)
        for plane in range(planes):
            for chip in range(chips):
                both = jnp.concatenate([near[chip][plane, :, span], far[chip][plane, :, span]], axis=0)
                target = (plane * chips + chip) * 2 * local
                panel[target : target + 2 * local, span] = both
                if start == 0:
                    code = pl.ds(columns, LANES)
                    both = jnp.concatenate([near[chip][plane, :, code], far[chip][plane, :, code]], axis=0)
                    member[target : target + 2 * local, :] = (both.astype(jnp.float32) == lanes).astype(jnp.bfloat16)
        sums = jnp.dot(ones, panel[:, span], preferred_element_type=jnp.float32)
        mean[:, span] = sums[:8] / total


def gram_kernel(pairs, first, tile, *refs):
    planes = len(pairs)
    parts, refs = refs[: sum(pairs)], refs[sum(pairs) :]
    panel, mean, member = refs[:3]
    cov, cross, rows_ref, out_ref, cross_ref, in_sem, out_sem, cross_sem = refs[-8:]
    _, _, col = place()
    total, columns = panel.shape
    shard, width = parts[0].shape
    slice_width = cross_ref.shape[1]
    chunk = out_ref.shape[2]

    def load(part, plane):
        return pltpu.make_async_copy(part, rows_ref.at[pl.ds(plane * shard, shard), :], in_sem.at[plane])

    index = 0
    for plane, count in enumerate(pairs):
        if count == 1:
            load(parts[index], plane).start()
        else:
            inside = (col > 0) & (col < planes - 1)
            pl.when(inside)(load(parts[index], plane).start)
            pl.when(jnp.logical_not(inside))(load(parts[index + 1], plane).start)
        index += count
    for plane in range(planes):
        load(parts[0], plane).wait()

    ones = jnp.ones((total, LANES), jnp.bfloat16)
    across = (((0,), (0,)), ((), ()))
    slots = out_ref.shape[0]
    per_row = columns // chunk
    steps = width // tile * per_row

    def store(step):
        slot = step % slots
        target = cov.at[pl.ds(first + step // per_row * tile, tile), pl.ds(step % per_row * chunk, chunk)]
        return pltpu.make_async_copy(out_ref.at[slot], target, out_sem.at[slot])

    for step in range(steps):
        if step >= slots:
            store(step - slots).wait()
        if step % per_row == 0:
            index = step // per_row
            left = rows_ref[:, index * tile : (index + 1) * tile]
            row_mean = lax.dot_general(left, ones, across, preferred_element_type=jnp.float32)[:, :1] / total
            left = left.T
        span = pl.ds(step % per_row * chunk, chunk)
        gram = jnp.dot(left, panel[:, span], preferred_element_type=jnp.float32)
        out_ref[step % slots] = gram * (1.0 / total) - row_mean * mean[:1, span]
        store(step).start()

    begin = col * slice_width - first
    mine = (begin >= 0) & (begin < width)
    save = pltpu.make_async_copy(cross_ref, cross, cross_sem)

    @pl.when(mine)
    def _():
        features = rows_ref[:, pl.ds(pl.multiple_of(begin, LANES), slice_width)]
        sums = lax.dot_general(member[...], features, across, preferred_element_type=jnp.float32)
        counts = lax.dot_general(member[...], ones, across, preferred_element_type=jnp.float32)[:, :1]
        slice_mean = jnp.dot(jnp.ones((16, total), jnp.bfloat16), features, preferred_element_type=jnp.float32)[:1] / total
        groups = member.shape[1]
        cross_ref[...] = (groups / total) * (sums - counts * slice_mean)
        save.start()

    for step in range(max(0, steps - slots), steps):
        store(step).wait()
    pl.when(mine)(save.wait)


def gram(own, received, panel, mean, member, first, outs):
    total, columns = panel.shape
    shard, width = own.shape
    tile = min(256, width)
    chunk = min(1024, columns)
    groups = [(own,)] + [part if isinstance(part, tuple) else (part,) for part in received]
    parts = [part for group in groups for part in group]
    inputs = [*parts, panel, mean, member]
    specs = [ANY] * len(parts) + [WHOLE] * 3
    aliases = {}
    if first:
        aliases = {len(inputs): 0, len(inputs) + 1: 1}
        inputs += outs
        specs += [ANY] * 2
    cov, cross = outs
    return pl.pallas_call(
        functools.partial(gram_kernel, tuple(map(len, groups)), first, tile),
        out_shape=[jax.ShapeDtypeStruct(cov.shape, cov.dtype), jax.ShapeDtypeStruct(cross.shape, cross.dtype)],
        in_specs=specs,
        out_specs=[ANY, ANY],
        scratch_shapes=[
            pltpu.VMEM((total, width), jnp.bfloat16),
            pltpu.VMEM((6, tile, chunk), jnp.float32),
            pltpu.VMEM(cross.shape, jnp.float32),
            pltpu.SemaphoreType.DMA((len(groups),)),
            pltpu.SemaphoreType.DMA((6,)),
            pltpu.SemaphoreType.DMA,
        ],
        input_output_aliases=aliases,
        compiler_params=params(24),
        cost_estimate=COST,
    )(*inputs)


def kernel(body, shapes, inputs, specs=None, mib=8):
    return pl.pallas_call(
        body,
        out_shape=[jax.ShapeDtypeStruct(shape, dtype) for shape, dtype in shapes],
        in_specs=specs or [WHOLE] * len(inputs),
        out_specs=[WHOLE] * len(shapes),
        compiler_params=params(mib),
        cost_estimate=COST,
    )(*inputs)


def gather_line(pieces, shard):
    half = shard.shape[0] // 2
    with jax.named_scope("planes_far"):
        far = [swap_cols(piece, 2) for piece in pieces]
    with jax.named_scope("planes_near"):
        near = [swap_cols(piece, 1) for piece in pieces]
    with jax.named_scope("chips_near"):
        sides = [swap_rows(shard, 2), swap_rows(shard, 4)]
    outer, inner, last = [], [], []
    (far[0], near[0], first), sides = lax.optimization_barrier(((far[0], near[0], pieces[0]), sides))
    with jax.named_scope("planes_last"):
        outer.append(swap_cols(far[0], 1))
        inner.append(pair_cols(first, 1))
    with jax.named_scope("chips_far"):
        corner = [swap_rows(sides[1][:half], 2), swap_rows(sides[0][half:], 4)]
    with jax.named_scope("cores"):
        others = [swap_rows(part, 1) for part in (shard, *sides)]
    (far[1], near[1], second), corner = lax.optimization_barrier(((far[1], near[1], pieces[1]), corner))
    with jax.named_scope("planes_last"):
        outer.append(swap_cols(far[1], 1))
        inner.append(pair_cols(second, 1))
    corner = jnp.concatenate(corner, axis=0)
    with jax.named_scope("cores"):
        others.append(swap_rows(corner, 1))
    arrays = [[near[i], far[i], (inner[i], outer[i])] for i in range(2)]
    return arrays, [shard, *sides, corner], others


def gather(pieces, shard):
    chips = lax.axis_size("row") // 2
    planes = lax.axis_size("col")
    if chips == 4 and planes == 4:
        return gather_line(pieces, shard)
    arrays = [[swap_cols(piece, mask) for mask in range(1, planes)] for piece in pieces]
    shards = [shard] + [swap_rows(shard, 2 * mask) for mask in range(1, chips)]
    return arrays, shards, [swap_rows(part, 1) for part in shards]


def shards(activations, tenant_ids, concept_labels):
    local, width = activations.shape
    rows = lax.axis_size("row")
    planes = lax.axis_size("col")
    chips = rows // 2
    block = width // rows
    panel_width = width // planes
    total = local * rows * planes
    groups = TENANTS * LABELS
    half = jnp.bfloat16

    dealt = kernel(
        functools.partial(deal_kernel, chips),
        [((local, 2 * block), half)] * chips + [((local, panel_width + LANES), half)] * planes,
        [tenant_ids, concept_labels, activations],
        [SCALARS, SCALARS, WHOLE],
    )
    to_rows, to_cols = dealt[:chips], dealt[chips:]
    col_parts = [to_cols[0]] + [swap_cols(to_cols[mask], mask) for mask in range(1, planes)]
    row_parts = [to_rows[0]] + [swap_rows(to_rows[mask], 2 * mask) for mask in range(1, chips)]
    (shared,) = kernel(share_kernel, [((chips, local, block), half)], row_parts)
    shared = swap_rows(shared, 1)

    slice_width = block // planes
    cut = slice_width * (planes // 4)
    pieces = kernel(
        functools.partial(rows_kernel, chips),
        [((rows * local, cut), half), ((rows * local, block - cut), half)],
        [*row_parts, shared],
    )
    (col_shard,) = kernel(stack_kernel, [((planes, local, panel_width + LANES), half)], col_parts)
    *pieces, col_shard = lax.optimization_barrier((*pieces, col_shard))
    chains, near, far = gather(pieces, col_shard)
    panel, mean, member = kernel(
        functools.partial(column_kernel, chips),
        [((total, panel_width), half), ((8, panel_width), jnp.float32), ((total, groups), half)],
        [*near, *far],
        mib=24,
    )

    outs = (
        jax.ShapeDtypeStruct((block, panel_width), jnp.float32),
        jax.ShapeDtypeStruct((groups, slice_width), jnp.float32),
    )
    first = 0
    for piece, arrays in zip(pieces, chains):
        outs = gram(piece, arrays, panel, mean, member, first, outs)
        first += piece.shape[1]
    return tuple(outs)


def solution(mesh):
    placed = (P(("row", "col"), None), P(("row", "col")), P(("row", "col")))
    return jax.shard_map(
        shards,
        mesh=mesh,
        in_specs=placed,
        out_specs=(P("row", "col"), P(None, ("row", "col"))),
        check_vma=False,
    )
```

```python
import functools

import jax
import jax.numpy as jnp
from jax import lax
from jax.experimental import pallas as pl
from jax.experimental.pallas import tpu as pltpu
from jax.sharding import PartitionSpec as P

TENANTS = 64
LABELS = 2
LANES = 128
MIB = 1024 * 1024

COST = pl.CostEstimate(flops=0, bytes_accessed=0, transcendentals=0)

ANY = pl.BlockSpec(memory_space=pl.ANY)
WHOLE = pl.BlockSpec(memory_space=pltpu.VMEM)


def params(mib):
    return pltpu.CompilerParams(vmem_limit_bytes=mib * MIB)


def swap_rows(x, mask):
    return lax.ppermute(x, "row", [(i, i ^ mask) for i in range(lax.axis_size("row"))])


def swap_cols(x, mask):
    return lax.ppermute(x, "col", [(i, i ^ mask) for i in range(lax.axis_size("col"))])


def pair_cols(x, first):
    count = lax.axis_size("col")
    partner = {i: i for i in range(count)}
    for low in range(first, count - 1, 2):
        partner[low], partner[low + 1] = low + 1, low
    return lax.ppermute(x, "col", list(partner.items()))


def place():
    row = lax.axis_index("row")
    return row // 2, row % 2, lax.axis_index("col")


def deal_kernel(chips, tenants_hbm, labels_hbm, features_hbm, *refs):
    *outs, features, tenants, labels, sems = refs
    loads = [
        pltpu.make_async_copy(features_hbm, features, sems.at[0]),
        pltpu.make_async_copy(tenants_hbm, tenants, sems.at[1]),
        pltpu.make_async_copy(labels_hbm, labels, sems.at[2]),
    ]
    for load in loads:
        load.start()
    for load in loads:
        load.wait()
    local, total = features.shape
    chip, _, col = place()
    row_outs, col_outs = outs[:chips], outs[chips:]
    width = total // len(col_outs)
    token = lax.broadcasted_iota(jnp.int32, (local, LANES), 0)
    codes = jnp.zeros((local, LANES), jnp.int32)
    for index in range(local):
        codes = jnp.where(token == index, tenants[index] * LABELS + labels[index], codes)
    codes = codes.astype(jnp.float32).astype(jnp.bfloat16)
    for mask, out in enumerate(col_outs):
        start = pl.multiple_of((col ^ mask) * width, LANES)
        out[:, :width] = features[:, pl.ds(start, width)]
        out[:, width:] = codes
    for mask, out in enumerate(row_outs):
        block = out.shape[1]
        start = pl.multiple_of((chip ^ mask) * block, LANES)
        out[...] = features[:, pl.ds(start, block)]


def share_kernel(*refs):
    *parts, out = refs
    _, core, _ = place()
    width = out.shape[2]
    start = pl.multiple_of((1 - core) * width, LANES)
    for index, part in enumerate(parts):
        out[index] = part[:, pl.ds(start, width)]


def rows_kernel(*refs):
    *parts, shared, out = refs
    _, core, _ = place()
    local, width = shared.shape[1:]
    begin = pl.multiple_of(core * width, LANES)
    for index, part in enumerate(parts):
        both = jnp.concatenate([part[:, pl.ds(begin, width)], shared[index]], axis=0)
        out[index * 2 * local : (index + 1) * 2 * local, :] = both


def cut_kernel(arrays, *refs):
    outs = refs[arrays:]
    for index, array in enumerate(refs[:arrays]):
        start = 0
        for out in outs[index * len(outs) // arrays : (index + 1) * len(outs) // arrays]:
            out[...] = array[:, start : start + out.shape[1]]
            start += out.shape[1]


def stack_kernel(*refs):
    *parts, out = refs
    start = 0
    for part in parts:
        rows = part.shape[0]
        out[start : start + rows] = part[...]
        start += rows


def column_kernel(chips, *refs):
    near, far, panel, mean, member, counts = refs
    total, columns = panel.shape
    _, local, _ = near.shape
    planes = near.shape[0] // chips
    step = min(512, columns)
    ones = jnp.ones((16, total), jnp.bfloat16)
    lanes = lax.broadcasted_iota(jnp.int32, (2 * local, LANES), 1).astype(jnp.float32)
    for start in range(0, columns, step):
        span = pl.ds(start, step)
        for plane in range(planes):
            for chip in range(chips):
                both = jnp.concatenate([near[chip * planes + plane, :, span], far[chip * planes + plane, :, span]], axis=0)
                target = (plane * chips + chip) * 2 * local
                panel[target : target + 2 * local, span] = both
                if start == 0:
                    code = pl.ds(columns, LANES)
                    both = jnp.concatenate([near[chip * planes + plane, :, code], far[chip * planes + plane, :, code]], axis=0)
                    member[target : target + 2 * local, :] = (both.astype(jnp.float32) == lanes).astype(jnp.bfloat16)
        sums = jnp.dot(ones, panel[:, span], preferred_element_type=jnp.float32)
        mean[:, span] = sums[:8] / total
    ones = jnp.ones((total, LANES), jnp.bfloat16)
    counts[...] = lax.dot_general(member[...], ones, (((0,), (0,)), ((), ())), preferred_element_type=jnp.float32)


def gram_kernel(pairs, first, tile, *refs):
    parts, refs = refs[: sum(pairs)], refs[sum(pairs) :]
    panel, mean, member, counts = refs[:4]
    cov, cross, left_ref, out_ref, cross_ref, out_sem, cross_sem = refs[-7:]
    _, _, col = place()
    total, columns = panel.shape
    width = left_ref.shape[0]
    slice_width = cross_ref.shape[1]
    chunk = out_ref.shape[2]
    inside = (col > 0) & (col < len(pairs) - 1)

    def features(start, size):
        blocks, index = [], 0
        for count in pairs:
            both = []
            for part in parts[index : index + count]:
                offset = first if part.shape[1] > width else 0
                both.append(part[:, pl.ds(start + offset, size)])
            blocks.append(both[0] if count == 1 else jnp.where(inside, both[0], both[1]))
            index += count
        return jnp.concatenate(blocks, axis=0)

    slots = out_ref.shape[0]
    per_row = columns // chunk
    steps = width // tile * per_row

    def store(step):
        slot = step % slots
        target = cov.at[pl.ds(first + step // per_row * tile, tile), pl.ds(step % per_row * chunk, chunk)]
        return pltpu.make_async_copy(out_ref.at[slot], target, out_sem.at[slot])

    for start in range(0, width, tile):
        left_ref[start : start + tile, :] = features(start, tile).T
    ones = jnp.ones((total, LANES), jnp.bfloat16)
    for step in range(steps):
        if step >= slots:
            store(step - slots).wait()
        left = left_ref[pl.ds(step // per_row * tile, tile), :]
        if step % per_row == 0:
            row_mean = jnp.dot(left, ones, preferred_element_type=jnp.float32)[:, :1] / total
        span = pl.ds(step % per_row * chunk, chunk)
        gram = jnp.dot(left, panel[:, span], preferred_element_type=jnp.float32)
        out_ref[step % slots] = gram * (1.0 / total) - row_mean * mean[:1, span]
        store(step).start()

    begin = col * slice_width - first
    mine = (begin >= 0) & (begin < width)
    save = pltpu.make_async_copy(cross_ref, cross, cross_sem)

    @pl.when(mine)
    def _():
        own = features(pl.multiple_of(begin, LANES), slice_width)
        sums = lax.dot_general(member[...], own, (((0,), (0,)), ((), ())), preferred_element_type=jnp.float32)
        slice_mean = jnp.dot(jnp.ones((16, total), jnp.bfloat16), own, preferred_element_type=jnp.float32)[:1] / total
        groups = member.shape[1]
        cross_ref[...] = (groups / total) * (sums - counts[:, :1] * slice_mean)
        save.start()

    for step in range(max(0, steps - slots), steps):
        store(step).wait()
    pl.when(mine)(save.wait)


def gram(groups, panel, mean, member, counts, first, width, outs):
    total, columns = panel.shape
    tile = min(256, width)
    chunk = min(2048, columns)
    slots = min(8, width // tile * (columns // chunk))
    parts = [part for group in groups for part in group]
    inputs = [*parts, panel, mean, member, counts]
    specs = [WHOLE] * len(inputs)
    aliases = {}
    if first:
        aliases = {len(inputs): 0, len(inputs) + 1: 1}
        inputs += outs
        specs += [ANY] * 2
    cov, cross = outs
    return pl.pallas_call(
        functools.partial(gram_kernel, tuple(map(len, groups)), first, tile),
        out_shape=[jax.ShapeDtypeStruct(cov.shape, cov.dtype), jax.ShapeDtypeStruct(cross.shape, cross.dtype)],
        in_specs=specs,
        out_specs=[ANY, ANY],
        scratch_shapes=[
            pltpu.VMEM((width, total), jnp.bfloat16),
            pltpu.VMEM((slots, tile, chunk), jnp.float32),
            pltpu.VMEM(cross.shape, jnp.float32),
            pltpu.SemaphoreType.DMA((slots,)),
            pltpu.SemaphoreType.DMA,
        ],
        input_output_aliases=aliases,
        compiler_params=params(40),
        cost_estimate=pl.CostEstimate(flops=0, bytes_accessed=2 * MIB, transcendentals=0),
    )(*inputs)


def kernel(body, shapes, inputs, specs=None, mib=8, scratch=(), cost=COST):
    return pl.pallas_call(
        body,
        out_shape=[jax.ShapeDtypeStruct(shape, dtype) for shape, dtype in shapes],
        in_specs=specs or [WHOLE] * len(inputs),
        out_specs=[WHOLE] * len(shapes),
        scratch_shapes=scratch,
        compiler_params=params(mib),
        cost_estimate=cost,
    )(*inputs)


def gather_line(rows, shard, widths):
    with jax.named_scope("planes_far"):
        far = swap_cols(rows, 2)
    with jax.named_scope("planes_near"):
        near = swap_cols(rows, 1)
    with jax.named_scope("chips"):
        shards = [shard] + [swap_rows(shard, 2 * mask) for mask in (1, 2, 3)]
    shards, rows, near, far = lax.optimization_barrier((shards, rows, near, far))
    cuts = kernel(functools.partial(cut_kernel, 2), [((rows.shape[0], width), rows.dtype) for width in widths] * 2, [rows, far])
    (stacked,) = kernel(stack_kernel, [((4 * shard.shape[0], *shard.shape[1:]), shard.dtype)], shards)
    with jax.named_scope("cores"):
        other = swap_rows(stacked, 1)
    groups = []
    for index in range(len(widths)):
        own, passed = cuts[index :: len(widths)]
        with jax.named_scope("planes_last"):
            last = (pair_cols(own, 1), swap_cols(passed, 1))
        groups.append([(rows,), (near,), (far,), last])
    return groups, stacked, other


def gather(rows, shard, widths):
    chips = lax.axis_size("row") // 2
    planes = lax.axis_size("col")
    if chips == 4 and planes == 4:
        return gather_line(rows, shard, widths)
    arrays = [(rows,)] + [(swap_cols(rows, mask),) for mask in range(1, planes)]
    shards = [shard] + [swap_rows(shard, 2 * mask) for mask in range(1, chips)]
    (stacked,) = kernel(stack_kernel, [((chips * shard.shape[0], *shard.shape[1:]), shard.dtype)], shards, mib=40)
    return [arrays] * len(widths), stacked, swap_rows(stacked, 1)


def shards(activations, tenant_ids, concept_labels):
    local, width = activations.shape
    rows = lax.axis_size("row")
    planes = lax.axis_size("col")
    chips = rows // 2
    block = width // rows
    panel_width = width // planes
    total = local * rows * planes
    groups = TENANTS * LABELS
    half = jnp.bfloat16

    dealt = kernel(
        functools.partial(deal_kernel, chips),
        [((local, 2 * block), half)] * chips + [((local, panel_width + LANES), half)] * planes,
        [tenant_ids, concept_labels, activations],
        [ANY, ANY, ANY],
        scratch=[
            pltpu.VMEM((local, width), half),
            pltpu.SMEM((local,), jnp.int32),
            pltpu.SMEM((local,), jnp.int32),
            pltpu.SemaphoreType.DMA((3,)),
        ],
    )
    to_rows, to_cols = dealt[:chips], dealt[chips:]
    col_parts = [to_cols[0]] + [swap_cols(to_cols[mask], mask) for mask in range(1, planes)]
    row_parts = [to_rows[0]] + [swap_rows(to_rows[mask], 2 * mask) for mask in range(1, chips)]
    row_parts, col_parts = lax.optimization_barrier((row_parts, col_parts))
    (shared,) = kernel(share_kernel, [((chips, local, block), half)], row_parts)
    shared = swap_rows(shared, 1)

    slice_width = block // planes
    cut = slice_width * (planes // 2)
    widths = (cut, block - cut)
    (row_shard,) = kernel(rows_kernel, [((rows * local, block), half)], [*row_parts, shared])
    shard_shape = (planes, local, panel_width + LANES)
    col_parts = [part.reshape(1, *part.shape) for part in col_parts]
    (col_shard,) = kernel(stack_kernel, [(shard_shape, half)], col_parts)

    pieces, near, far = gather(row_shard, col_shard, widths)
    panel, mean, member, counts = kernel(
        functools.partial(column_kernel, chips),
        [((total, panel_width), half), ((8, panel_width), jnp.float32), ((total, groups), half), ((groups, LANES), jnp.float32)],
        [near, far],
        mib=40,
    )

    outs = (
        jax.ShapeDtypeStruct((block, panel_width), jnp.float32),
        jax.ShapeDtypeStruct((groups, slice_width), jnp.float32),
    )
    first = 0
    for piece, piece_width in zip(pieces, widths):
        outs = gram(piece, panel, mean, member, counts, first, piece_width, outs)
        first += piece_width
    return tuple(outs)


def solution(mesh):
    placed = (P(("row", "col"), None), P(("row", "col")), P(("row", "col")))
    return jax.shard_map(
        shards,
        mesh=mesh,
        in_specs=placed,
        out_specs=(P("row", "col"), P(None, ("row", "col"))),
        check_vma=False,
    )
```

```python
import functools

import jax
import jax.numpy as jnp
from jax import lax
from jax.experimental import pallas as pl
from jax.experimental.pallas import tpu as pltpu
from jax.sharding import PartitionSpec as P

TENANTS = 64
LABELS = 2
LANES = 128
MIB = 1024 * 1024

COST = pl.CostEstimate(flops=0, bytes_accessed=0, transcendentals=0)

ANY = pl.BlockSpec(memory_space=pl.ANY)
WHOLE = pl.BlockSpec(memory_space=pltpu.VMEM)


def params(mib):
    return pltpu.CompilerParams(vmem_limit_bytes=mib * MIB)


def swap_rows(x, mask):
    return lax.ppermute(x, "row", [(i, i ^ mask) for i in range(lax.axis_size("row"))])


def swap_cols(x, mask):
    return lax.ppermute(x, "col", [(i, i ^ mask) for i in range(lax.axis_size("col"))])


def pair_cols(x, first):
    count = lax.axis_size("col")
    partner = {i: i for i in range(count)}
    for low in range(first, count - 1, 2):
        partner[low], partner[low + 1] = low + 1, low
    return lax.ppermute(x, "col", list(partner.items()))


def place():
    row = lax.axis_index("row")
    return row // 2, row % 2, lax.axis_index("col")


def deal_kernel(chips, codes_hbm, features_hbm, *refs):
    *outs, features, groups, sems = refs
    loads = [
        pltpu.make_async_copy(features_hbm, features, sems.at[0]),
        pltpu.make_async_copy(codes_hbm, groups, sems.at[1]),
    ]
    for load in loads:
        load.start()
    for load in loads:
        load.wait()
    local, total = features.shape
    chip, _, col = place()
    row_outs, col_outs = outs[:chips], outs[chips:]
    width = total // len(col_outs)
    token = lax.broadcasted_iota(jnp.int32, (local, LANES), 0)
    codes = jnp.zeros((local, LANES), jnp.int32)
    for index in range(local):
        codes = jnp.where(token == index, groups[index], codes)
    codes = codes.astype(jnp.float32).astype(jnp.bfloat16)
    for mask, out in enumerate(col_outs):
        start = pl.multiple_of((col ^ mask) * width, LANES)
        out[:, :width] = features[:, pl.ds(start, width)]
        out[:, width:] = codes
    for mask, out in enumerate(row_outs):
        block = out.shape[1]
        start = pl.multiple_of((chip ^ mask) * block, LANES)
        out[...] = features[:, pl.ds(start, block)]


def share_kernel(*refs):
    *parts, out = refs
    _, core, _ = place()
    width = out.shape[2]
    start = pl.multiple_of((1 - core) * width, LANES)
    for index, part in enumerate(parts):
        out[index] = part[:, pl.ds(start, width)]


def rows_kernel(*refs):
    *parts, shared, out = refs
    _, core, _ = place()
    local, width = shared.shape[1:]
    begin = pl.multiple_of(core * width, LANES)
    for index, part in enumerate(parts):
        both = jnp.concatenate([part[:, pl.ds(begin, width)], shared[index]], axis=0)
        out[index * 2 * local : (index + 1) * 2 * local, :] = both


def cut_kernel(arrays, *refs):
    outs = refs[arrays:]
    for index, array in enumerate(refs[:arrays]):
        start = 0
        for out in outs[index * len(outs) // arrays : (index + 1) * len(outs) // arrays]:
            out[...] = array[:, start : start + out.shape[1]]
            start += out.shape[1]


def stack_kernel(*refs):
    *parts, out = refs
    start = 0
    for part in parts:
        rows = part.shape[0]
        out[start : start + rows] = part[...]
        start += rows


def column_kernel(chips, *refs):
    near, far, panel, mean, member, counts = refs
    total, columns = panel.shape
    _, local, _ = near.shape
    planes = near.shape[0] // chips
    step = min(512, columns)
    ones = jnp.ones((16, total), jnp.bfloat16)
    lanes = lax.broadcasted_iota(jnp.int32, (2 * local, LANES), 1).astype(jnp.float32)
    for start in range(0, columns, step):
        span = pl.ds(start, step)
        for plane in range(planes):
            for chip in range(chips):
                both = jnp.concatenate([near[chip * planes + plane, :, span], far[chip * planes + plane, :, span]], axis=0)
                target = (plane * chips + chip) * 2 * local
                panel[target : target + 2 * local, span] = both
                if start == 0:
                    code = pl.ds(columns, LANES)
                    both = jnp.concatenate([near[chip * planes + plane, :, code], far[chip * planes + plane, :, code]], axis=0)
                    member[target : target + 2 * local, :] = (both.astype(jnp.float32) == lanes).astype(jnp.bfloat16)
        sums = jnp.dot(ones, panel[:, span], preferred_element_type=jnp.float32)
        mean[:, span] = sums[:8] / total
    ones = jnp.ones((total, LANES), jnp.bfloat16)
    counts[...] = lax.dot_general(member[...], ones, (((0,), (0,)), ((), ())), preferred_element_type=jnp.float32)


def gram_kernel(pairs, first, tile, *refs):
    parts, refs = refs[: sum(pairs)], refs[sum(pairs) :]
    panel, mean, member, counts = refs[:4]
    cov, cross, left_ref, out_ref, cross_ref, out_sem, cross_sem = refs[-7:]
    _, _, col = place()
    total, columns = panel.shape
    width = left_ref.shape[0]
    slice_width = cross_ref.shape[1]
    chunk = out_ref.shape[2]
    inside = (col > 0) & (col < len(pairs) - 1)

    def features(start, size):
        blocks, index = [], 0
        for count in pairs:
            both = []
            for part in parts[index : index + count]:
                offset = first if part.shape[1] > width else 0
                both.append(part[:, pl.ds(start + offset, size)])
            blocks.append(both[0] if count == 1 else jnp.where(inside, both[1], both[0]))
            index += count
        return jnp.concatenate(blocks, axis=0)

    slots = out_ref.shape[0]
    per_row = columns // chunk
    steps = width // tile * per_row

    def store(step):
        slot = step % slots
        target = cov.at[pl.ds(first + step // per_row * tile, tile), pl.ds(step % per_row * chunk, chunk)]
        return pltpu.make_async_copy(out_ref.at[slot], target, out_sem.at[slot])

    ones = jnp.ones((total, LANES), jnp.bfloat16)
    for step in range(steps):
        if step >= slots:
            store(step - slots).wait()
        rows = pl.ds(step // per_row * tile, tile)
        if step % per_row == 0:
            left = features(step // per_row * tile, tile).T
            left_ref[rows, :] = left
            row_mean = jnp.dot(left, ones, preferred_element_type=jnp.float32)[:, :1] / total
        span = pl.ds(step % per_row * chunk, chunk)
        gram = jnp.dot(left_ref[rows, :], panel[:, span], preferred_element_type=jnp.float32)
        out_ref[step % slots] = gram * (1.0 / total) - row_mean * mean[:1, span]
        store(step).start()

    begin = col * slice_width - first
    mine = (begin >= 0) & (begin < width)
    save = pltpu.make_async_copy(cross_ref, cross, cross_sem)

    @pl.when(mine)
    def _():
        own = features(pl.multiple_of(begin, LANES), slice_width)
        sums = lax.dot_general(member[...], own, (((0,), (0,)), ((), ())), preferred_element_type=jnp.float32)
        slice_mean = jnp.dot(jnp.ones((16, total), jnp.bfloat16), own, preferred_element_type=jnp.float32)[:1] / total
        groups = member.shape[1]
        cross_ref[...] = (groups / total) * (sums - counts[:, :1] * slice_mean)
        save.start()

    for step in range(max(0, steps - slots), steps):
        store(step).wait()
    pl.when(mine)(save.wait)


def gram(groups, panel, mean, member, counts, first, width, outs):
    total, columns = panel.shape
    tile = min(256, width)
    chunk = min(1024, columns)
    slots = min(16, width // tile * (columns // chunk))
    parts = [part for group in groups for part in group]
    inputs = [*parts, panel, mean, member, counts]
    specs = [WHOLE] * len(inputs)
    aliases = {}
    if first:
        aliases = {len(inputs): 0, len(inputs) + 1: 1}
        inputs += outs
        specs += [ANY] * 2
    cov, cross = outs
    return pl.pallas_call(
        functools.partial(gram_kernel, tuple(map(len, groups)), first, tile),
        out_shape=[jax.ShapeDtypeStruct(cov.shape, cov.dtype), jax.ShapeDtypeStruct(cross.shape, cross.dtype)],
        in_specs=specs,
        out_specs=[ANY, ANY],
        scratch_shapes=[
            pltpu.VMEM((width, total), jnp.bfloat16),
            pltpu.VMEM((slots, tile, chunk), jnp.float32),
            pltpu.VMEM(cross.shape, jnp.float32),
            pltpu.SemaphoreType.DMA((slots,)),
            pltpu.SemaphoreType.DMA,
        ],
        input_output_aliases=aliases,
        compiler_params=params(25),
        cost_estimate=pl.CostEstimate(flops=0, bytes_accessed=2 * MIB, transcendentals=0),
    )(*inputs)


def early_kernel(first, tile, *refs):
    *parts, panel, acc, sums, left_ref = refs
    width, depth = left_ref.shape
    columns = panel.shape[1]
    chunk = min(1024, columns)
    ones = jnp.ones((depth, LANES), jnp.bfloat16)
    for start in range(0, width, tile):
        rows = pl.ds(start, tile)
        left = jnp.concatenate([part[:, pl.ds(first + start, tile)] for part in parts], axis=0).T
        left_ref[rows, :] = left
        sums[rows, :] = jnp.dot(left, ones, preferred_element_type=jnp.float32)
    for start in range(0, width, tile):
        rows = pl.ds(start, tile)
        for begin in range(0, columns, chunk):
            span = pl.ds(begin, chunk)
            acc[rows, span] = jnp.dot(left_ref[rows, :], panel[:depth, span], preferred_element_type=jnp.float32)


def early(parts, panel, first, width):
    shard = parts[0].shape[0]
    depth = shard * len(parts)
    return kernel(
        functools.partial(early_kernel, first, min(256, width)),
        [((width, panel.shape[1]), jnp.float32), ((width, LANES), jnp.float32)],
        [*parts, panel],
        mib=10,
        scratch=[pltpu.VMEM((width, depth), jnp.bfloat16)],
    )


def late_kernel(count, first, tile, *refs):
    parts, last, refs = refs[: count[0]], refs[count[0] : sum(count)], refs[sum(count) :]
    acc, sums, panel, mean, member, counts = refs[:6]
    cov, cross, left_ref, out_ref, cross_ref, out_sem, cross_sem = refs[-7:]
    _, _, col = place()
    total, columns = panel.shape
    width, depth = left_ref.shape
    slice_width = cross_ref.shape[1]
    chunk = out_ref.shape[2]
    inside = (col > 0) & (col < count[0])

    def latest(start, size):
        both = [part[:, pl.ds(start, size)] for part in last]
        return both[0] if len(both) == 1 else jnp.where(inside, both[1], both[0])

    slots = out_ref.shape[0]
    per_row = columns // chunk
    steps = width // tile * per_row

    def store(step):
        slot = step % slots
        target = cov.at[pl.ds(first + step // per_row * tile, tile), pl.ds(step % per_row * chunk, chunk)]
        return pltpu.make_async_copy(out_ref.at[slot], target, out_sem.at[slot])

    ones = jnp.ones((depth, LANES), jnp.bfloat16)
    for step in range(steps):
        if step >= slots:
            store(step - slots).wait()
        rows = pl.ds(step // per_row * tile, tile)
        if step % per_row == 0:
            left = latest(step // per_row * tile, tile).T
            left_ref[rows, :] = left
            row_sum = sums[rows, :] + jnp.dot(left, ones, preferred_element_type=jnp.float32)
            row_mean = row_sum[:, :1] / total
        span = pl.ds(step % per_row * chunk, chunk)
        gram = acc[rows, span] + jnp.dot(left_ref[rows, :], panel[total - depth :, span], preferred_element_type=jnp.float32)
        out_ref[step % slots] = gram * (1.0 / total) - row_mean * mean[:1, span]
        store(step).start()

    begin = col * slice_width - first
    mine = (begin >= 0) & (begin < width)
    save = pltpu.make_async_copy(cross_ref, cross, cross_sem)

    @pl.when(mine)
    def _():
        place_in_row = pl.multiple_of(col * slice_width, LANES)
        blocks = [part[:, pl.ds(place_in_row, slice_width)] for part in parts]
        own = jnp.concatenate([*blocks, latest(pl.multiple_of(begin, LANES), slice_width)], axis=0)
        group_sums = lax.dot_general(member[...], own, (((0,), (0,)), ((), ())), preferred_element_type=jnp.float32)
        slice_mean = jnp.dot(jnp.ones((16, total), jnp.bfloat16), own, preferred_element_type=jnp.float32)[:1] / total
        groups = member.shape[1]
        cross_ref[...] = (groups / total) * (group_sums - counts[:, :1] * slice_mean)
        save.start()

    for step in range(max(0, steps - slots), steps):
        store(step).wait()
    pl.when(mine)(save.wait)


def late(parts, last, part_gram, panel, mean, member, counts, first, outs):
    acc, sums = part_gram
    columns = panel.shape[1]
    width = acc.shape[0]
    tile = min(256, width)
    chunk = min(1024, columns)
    slots = min(8, width // tile * (columns // chunk))
    inputs = [*parts, *last, acc, sums, panel, mean, member, counts]
    specs = [WHOLE] * len(inputs)
    aliases = {}
    if first:
        aliases = {len(inputs): 0, len(inputs) + 1: 1}
        inputs += outs
        specs += [ANY] * 2
    cov, cross = outs
    return pl.pallas_call(
        functools.partial(late_kernel, (len(parts), len(last)), first, tile),
        out_shape=[jax.ShapeDtypeStruct(cov.shape, cov.dtype), jax.ShapeDtypeStruct(cross.shape, cross.dtype)],
        in_specs=specs,
        out_specs=[ANY, ANY],
        scratch_shapes=[
            pltpu.VMEM((width, last[0].shape[0]), jnp.bfloat16),
            pltpu.VMEM((slots, tile, chunk), jnp.float32),
            pltpu.VMEM(cross.shape, jnp.float32),
            pltpu.SemaphoreType.DMA((slots,)),
            pltpu.SemaphoreType.DMA,
        ],
        input_output_aliases=aliases,
        compiler_params=params(14),
        cost_estimate=pl.CostEstimate(flops=0, bytes_accessed=2 * MIB, transcendentals=0),
    )(*inputs)


def kernel(body, shapes, inputs, specs=None, mib=8, scratch=(), cost=COST):
    return pl.pallas_call(
        body,
        out_shape=[jax.ShapeDtypeStruct(shape, dtype) for shape, dtype in shapes],
        in_specs=specs or [WHOLE] * len(inputs),
        out_specs=[WHOLE] * len(shapes),
        scratch_shapes=scratch,
        compiler_params=params(mib),
        cost_estimate=cost,
    )(*inputs)


def gather_line(rows, shard, widths):
    with jax.named_scope("planes_far"):
        far = swap_cols(rows, 2)
    with jax.named_scope("planes_near"):
        near = swap_cols(rows, 1)
    with jax.named_scope("chips"):
        half = shard.shape[0] // 2
        sides = [swap_rows(shard, 2), swap_rows(shard, 4)]
        corner = [swap_rows(sides[1][:half], 2), swap_rows(sides[0][half:], 4)]
        shards = [shard, *sides, *corner]
    shards, rows, near, far = lax.optimization_barrier((shards, rows, near, far))
    cuts = kernel(functools.partial(cut_kernel, 2), [((rows.shape[0], width), rows.dtype) for width in widths] * 2, [rows, far])
    (stacked,) = kernel(stack_kernel, [((4 * shard.shape[0], *shard.shape[1:]), shard.dtype)], shards)
    with jax.named_scope("cores"):
        other = swap_rows(stacked, 1)
    groups = []
    for index in range(len(widths)):
        own, passed = cuts[index :: len(widths)]
        with jax.named_scope("planes_last"):
            last = (swap_cols(passed, 1), pair_cols(own, 1))
        groups.append([(rows,), (near,), (far,), last])
    return groups, stacked, other


def gather(rows, shard, widths):
    chips = lax.axis_size("row") // 2
    planes = lax.axis_size("col")
    if chips == 4 and planes == 4:
        return gather_line(rows, shard, widths)
    arrays = [(rows,)] + [(swap_cols(rows, mask),) for mask in range(1, planes)]
    starts = [sum(widths[:index]) for index in range(len(widths))]
    last = [arrays[-1][0][:, start : start + width] for start, width in zip(starts, widths)]
    shards = [shard] + [swap_rows(shard, 2 * mask) for mask in range(1, chips)]
    (stacked,) = kernel(stack_kernel, [((chips * shard.shape[0], *shard.shape[1:]), shard.dtype)], shards, mib=40)
    return [[*arrays[:-1], (part,)] for part in last], stacked, swap_rows(stacked, 1)


def shards(activations, tenant_ids, concept_labels):
    local, width = activations.shape
    rows = lax.axis_size("row")
    planes = lax.axis_size("col")
    chips = rows // 2
    block = width // rows
    panel_width = width // planes
    total = local * rows * planes
    groups = TENANTS * LABELS
    half = jnp.bfloat16

    dealt = kernel(
        functools.partial(deal_kernel, chips),
        [((local, 2 * block), half)] * chips + [((local, panel_width + LANES), half)] * planes,
        [tenant_ids * LABELS + concept_labels, activations],
        [ANY, ANY],
        scratch=[
            pltpu.VMEM((local, width), half),
            pltpu.SMEM((local,), jnp.int32),
            pltpu.SemaphoreType.DMA((2,)),
        ],
    )
    to_rows, to_cols = dealt[:chips], dealt[chips:]
    col_parts = [to_cols[0]] + [swap_cols(to_cols[mask], mask) for mask in range(1, planes)]
    row_parts = [to_rows[0]] + [swap_rows(to_rows[mask], 2 * mask) for mask in range(1, chips)]
    row_parts, col_parts = lax.optimization_barrier((row_parts, col_parts))
    (shared,) = kernel(share_kernel, [((chips, local, block), half)], row_parts)
    shared = swap_rows(shared, 1)

    slice_width = block // planes
    cut = slice_width * (planes // 2)
    widths = (cut, block - cut)
    (row_shard,) = kernel(rows_kernel, [((rows * local, block), half)], [*row_parts, shared])
    shard_shape = (planes, local, panel_width + LANES)
    col_parts = [part.reshape(1, *part.shape) for part in col_parts]
    (col_shard,) = kernel(stack_kernel, [(shard_shape, half)], col_parts)

    pieces, near, far = gather(row_shard, col_shard, widths)
    panel, mean, member, counts = kernel(
        functools.partial(column_kernel, chips),
        [((total, panel_width), half), ((8, panel_width), jnp.float32), ((total, groups), half), ((groups, LANES), jnp.float32)],
        [near, far],
        mib=10,
    )

    outs = (
        jax.ShapeDtypeStruct((block, panel_width), jnp.float32),
        jax.ShapeDtypeStruct((groups, slice_width), jnp.float32),
    )
    (*parts, last), *others = pieces
    parts = [part for (part,) in parts]
    part_gram = early(parts, panel, 0, widths[0])
    outs = late(parts, last, part_gram, panel, mean, member, counts, 0, outs)
    first = widths[0]
    for piece, size in zip(others, widths[1:]):
        outs = gram(piece, panel, mean, member, counts, first, size, outs)
        first += size
    return tuple(outs)


def solution(mesh):
    placed = (P(("row", "col"), None), P(("row", "col")), P(("row", "col")))
    return jax.shard_map(
        shards,
        mesh=mesh,
        in_specs=placed,
        out_specs=(P("row", "col"), P(None, ("row", "col"))),
        check_vma=False,
    )
```

```python
import functools

import jax
import jax.numpy as jnp
from jax import lax
from jax.experimental import pallas as pl
from jax.experimental.pallas import tpu as pltpu
from jax.sharding import PartitionSpec as P

TENANTS = 64
LABELS = 2
LANES = 128
MIB = 1024 * 1024

COST = pl.CostEstimate(flops=0, bytes_accessed=0, transcendentals=0)

ANY = pl.BlockSpec(memory_space=pl.ANY)
WHOLE = pl.BlockSpec(memory_space=pltpu.VMEM)


def params(mib):
    return pltpu.CompilerParams(vmem_limit_bytes=mib * MIB)


def swap_rows(x, mask):
    return lax.ppermute(x, "row", [(i, i ^ mask) for i in range(lax.axis_size("row"))])


def swap_cols(x, mask):
    return lax.ppermute(x, "col", [(i, i ^ mask) for i in range(lax.axis_size("col"))])


def pair_cols(x, first):
    count = lax.axis_size("col")
    partner = {i: i for i in range(count)}
    for low in range(first, count - 1, 2):
        partner[low], partner[low + 1] = low + 1, low
    return lax.ppermute(x, "col", list(partner.items()))


def place():
    row = lax.axis_index("row")
    return row // 2, row % 2, lax.axis_index("col")


def deal_kernel(chips, codes_hbm, features_hbm, *refs):
    *outs, features, groups, sems = refs
    loads = [
        pltpu.make_async_copy(features_hbm, features, sems.at[0]),
        pltpu.make_async_copy(codes_hbm, groups, sems.at[1]),
    ]
    for load in loads:
        load.start()
    for load in loads:
        load.wait()
    local, total = features.shape
    chip, _, col = place()
    row_outs, col_outs = outs[:chips], outs[chips:]
    width = total // len(col_outs)
    token = lax.broadcasted_iota(jnp.int32, (local, LANES), 0)
    codes = jnp.zeros((local, LANES), jnp.int32)
    for index in range(local):
        codes = jnp.where(token == index, groups[index], codes)
    codes = codes.astype(jnp.float32).astype(jnp.bfloat16)
    for mask, out in enumerate(col_outs):
        start = pl.multiple_of((col ^ mask) * width, LANES)
        out[:, :width] = features[:, pl.ds(start, width)]
        out[:, width:] = codes
    for mask, out in enumerate(row_outs):
        block = out.shape[1]
        start = pl.multiple_of((chip ^ mask) * block, LANES)
        out[...] = features[:, pl.ds(start, block)]


def share_kernel(parts, *refs):
    _, core, _ = place()
    outs = refs[parts:]
    width = outs[0].shape[2]
    for side, out in enumerate(outs):
        start = pl.multiple_of(((1 - core) * len(outs) + side) * width, LANES)
        for index, part in enumerate(refs[:parts]):
            out[index] = part[:, pl.ds(start, width)]


def rows_kernel(parts, *refs):
    *shared, out = refs[parts:]
    _, core, _ = place()
    local, width = shared[0].shape[1:]
    begin = pl.multiple_of(core * out.shape[1], LANES)
    for index, part in enumerate(refs[:parts]):
        rows = pl.ds(index * 2 * local, 2 * local)
        for side, other in enumerate(shared):
            own = part[:, pl.ds(begin + side * width, width)]
            out[rows, side * width : (side + 1) * width] = jnp.concatenate([own, other[index]], axis=0)


def cut_kernel(arrays, *refs):
    outs = refs[arrays:]
    for index, array in enumerate(refs[:arrays]):
        start = 0
        for out in outs[index * len(outs) // arrays : (index + 1) * len(outs) // arrays]:
            out[...] = array[:, start : start + out.shape[1]]
            start += out.shape[1]


def stack_kernel(*refs):
    *parts, out = refs
    start = 0
    for part in parts:
        rows = part.shape[0]
        out[start : start + rows] = part[...]
        start += rows


def column_kernel(chips, *refs):
    near, far, panel, mean, member, counts = refs
    total, columns = panel.shape
    _, local, _ = near.shape
    planes = near.shape[0] // chips
    step = min(512, columns)
    ones = jnp.ones((16, total), jnp.bfloat16)
    lanes = lax.broadcasted_iota(jnp.int32, (2 * local, LANES), 1).astype(jnp.float32)
    for start in range(0, columns, step):
        span = pl.ds(start, step)
        for plane in range(planes):
            for chip in range(chips):
                both = jnp.concatenate([near[chip * planes + plane, :, span], far[chip * planes + plane, :, span]], axis=0)
                target = (plane * chips + chip) * 2 * local
                panel[target : target + 2 * local, span] = both
                if start == 0:
                    code = pl.ds(columns, LANES)
                    both = jnp.concatenate([near[chip * planes + plane, :, code], far[chip * planes + plane, :, code]], axis=0)
                    member[target : target + 2 * local, :] = (both.astype(jnp.float32) == lanes).astype(jnp.bfloat16)
        sums = jnp.dot(ones, panel[:, span], preferred_element_type=jnp.float32)
        mean[:, span] = sums[:8] / total
    ones = jnp.ones((total, LANES), jnp.bfloat16)
    counts[...] = lax.dot_general(member[...], ones, (((0,), (0,)), ((), ())), preferred_element_type=jnp.float32)


def gram_kernel(pairs, first, tile, *refs):
    parts, refs = refs[: sum(pairs)], refs[sum(pairs) :]
    panel, mean, member, counts = refs[:4]
    cov, cross, left_ref, out_ref, cross_ref, out_sem, cross_sem = refs[-7:]
    _, _, col = place()
    total, columns = panel.shape
    width = left_ref.shape[0]
    slice_width = cross_ref.shape[1]
    chunk = out_ref.shape[2]
    inside = (col > 0) & (col < len(pairs) - 1)

    def features(start, size):
        blocks, index = [], 0
        for count in pairs:
            both = []
            for part in parts[index : index + count]:
                offset = first if part.shape[1] > width else 0
                both.append(part[:, pl.ds(start + offset, size)])
            blocks.append(both[0] if count == 1 else jnp.where(inside, both[1], both[0]))
            index += count
        return jnp.concatenate(blocks, axis=0)

    slots = out_ref.shape[0]
    per_row = columns // chunk
    steps = width // tile * per_row

    def store(step):
        slot = step % slots
        target = cov.at[pl.ds(first + step // per_row * tile, tile), pl.ds(step % per_row * chunk, chunk)]
        return pltpu.make_async_copy(out_ref.at[slot], target, out_sem.at[slot])

    ones = jnp.ones((total, LANES), jnp.bfloat16)
    for step in range(steps):
        if step >= slots:
            store(step - slots).wait()
        rows = pl.ds(step // per_row * tile, tile)
        if step % per_row == 0:
            left = features(step // per_row * tile, tile).T
            left_ref[rows, :] = left
            row_mean = jnp.dot(left, ones, preferred_element_type=jnp.float32)[:, :1] / total
        span = pl.ds(step % per_row * chunk, chunk)
        gram = jnp.dot(left_ref[rows, :], panel[:, span], preferred_element_type=jnp.float32)
        out_ref[step % slots] = gram * (1.0 / total) - row_mean * mean[:1, span]
        store(step).start()

    begin = col * slice_width - first
    mine = (begin >= 0) & (begin < width)
    save = pltpu.make_async_copy(cross_ref, cross, cross_sem)

    @pl.when(mine)
    def _():
        own = features(pl.multiple_of(begin, LANES), slice_width)
        sums = lax.dot_general(member[...], own, (((0,), (0,)), ((), ())), preferred_element_type=jnp.float32)
        slice_mean = jnp.dot(jnp.ones((16, total), jnp.bfloat16), own, preferred_element_type=jnp.float32)[:1] / total
        groups = member.shape[1]
        cross_ref[...] = (groups / total) * (sums - counts[:, :1] * slice_mean)
        save.start()

    for step in range(max(0, steps - slots), steps):
        store(step).wait()
    pl.when(mine)(save.wait)


def gram(groups, panel, mean, member, counts, first, width, outs):
    total, columns = panel.shape
    tile = min(256, width)
    chunk = min(1024, columns)
    slots = min(16, width // tile * (columns // chunk))
    parts = [part for group in groups for part in group]
    inputs = [*parts, panel, mean, member, counts]
    specs = [WHOLE] * len(inputs)
    aliases = {}
    if first:
        aliases = {len(inputs): 0, len(inputs) + 1: 1}
        inputs += outs
        specs += [ANY] * 2
    cov, cross = outs
    return pl.pallas_call(
        functools.partial(gram_kernel, tuple(map(len, groups)), first, tile),
        out_shape=[jax.ShapeDtypeStruct(cov.shape, cov.dtype), jax.ShapeDtypeStruct(cross.shape, cross.dtype)],
        in_specs=specs,
        out_specs=[ANY, ANY],
        scratch_shapes=[
            pltpu.VMEM((width, total), jnp.bfloat16),
            pltpu.VMEM((slots, tile, chunk), jnp.float32),
            pltpu.VMEM(cross.shape, jnp.float32),
            pltpu.SemaphoreType.DMA((slots,)),
            pltpu.SemaphoreType.DMA,
        ],
        input_output_aliases=aliases,
        compiler_params=params(25),
        cost_estimate=pl.CostEstimate(flops=0, bytes_accessed=2 * MIB, transcendentals=0),
    )(*inputs)


def early_kernel(first, tile, *refs):
    *parts, panel, acc, sums, left_ref = refs
    width, depth = left_ref.shape
    columns = panel.shape[1]
    chunk = min(1024, columns)
    ones = jnp.ones((depth, LANES), jnp.bfloat16)
    for start in range(0, width, tile):
        rows = pl.ds(start, tile)
        left = jnp.concatenate([part[:, pl.ds(first + start, tile)] for part in parts], axis=0).T
        left_ref[rows, :] = left
        sums[rows, :] = jnp.dot(left, ones, preferred_element_type=jnp.float32)
    for start in range(0, width, tile):
        rows = pl.ds(start, tile)
        for begin in range(0, columns, chunk):
            span = pl.ds(begin, chunk)
            acc[rows, span] = jnp.dot(left_ref[rows, :], panel[:depth, span], preferred_element_type=jnp.float32)


def early(parts, panel, first, width):
    shard = parts[0].shape[0]
    depth = shard * len(parts)
    return kernel(
        functools.partial(early_kernel, first, min(256, width)),
        [((width, panel.shape[1]), jnp.float32), ((width, LANES), jnp.float32)],
        [*parts, panel],
        mib=10,
        scratch=[pltpu.VMEM((width, depth), jnp.bfloat16)],
    )


def late_kernel(count, first, tile, *refs):
    parts, last, refs = refs[: count[0]], refs[count[0] : sum(count)], refs[sum(count) :]
    acc, sums, panel, mean, member, counts = refs[:6]
    cov, cross, left_ref, out_ref, cross_ref, out_sem, cross_sem = refs[-7:]
    _, _, col = place()
    total, columns = panel.shape
    width, depth = left_ref.shape
    slice_width = cross_ref.shape[1]
    chunk = out_ref.shape[2]
    inside = (col > 0) & (col < count[0])

    def latest(start, size):
        both = [part[:, pl.ds(start, size)] for part in last]
        return both[0] if len(both) == 1 else jnp.where(inside, both[1], both[0])

    slots = out_ref.shape[0]
    per_row = columns // chunk
    steps = width // tile * per_row

    def store(step):
        slot = step % slots
        target = cov.at[pl.ds(first + step // per_row * tile, tile), pl.ds(step % per_row * chunk, chunk)]
        return pltpu.make_async_copy(out_ref.at[slot], target, out_sem.at[slot])

    ones = jnp.ones((depth, LANES), jnp.bfloat16)
    for step in range(steps):
        if step >= slots:
            store(step - slots).wait()
        rows = pl.ds(step // per_row * tile, tile)
        if step % per_row == 0:
            left = latest(step // per_row * tile, tile).T
            left_ref[rows, :] = left
            row_sum = sums[rows, :] + jnp.dot(left, ones, preferred_element_type=jnp.float32)
            row_mean = row_sum[:, :1] / total
        span = pl.ds(step % per_row * chunk, chunk)
        gram = acc[rows, span] + jnp.dot(left_ref[rows, :], panel[total - depth :, span], preferred_element_type=jnp.float32)
        out_ref[step % slots] = gram * (1.0 / total) - row_mean * mean[:1, span]
        store(step).start()

    begin = col * slice_width - first
    mine = (begin >= 0) & (begin < width)
    save = pltpu.make_async_copy(cross_ref, cross, cross_sem)

    @pl.when(mine)
    def _():
        place_in_row = pl.multiple_of(col * slice_width, LANES)
        blocks = [part[:, pl.ds(place_in_row, slice_width)] for part in parts]
        own = jnp.concatenate([*blocks, latest(pl.multiple_of(begin, LANES), slice_width)], axis=0)
        group_sums = lax.dot_general(member[...], own, (((0,), (0,)), ((), ())), preferred_element_type=jnp.float32)
        slice_mean = jnp.dot(jnp.ones((16, total), jnp.bfloat16), own, preferred_element_type=jnp.float32)[:1] / total
        groups = member.shape[1]
        cross_ref[...] = (groups / total) * (group_sums - counts[:, :1] * slice_mean)
        save.start()

    for step in range(max(0, steps - slots), steps):
        store(step).wait()
    pl.when(mine)(save.wait)


def late(parts, last, part_gram, panel, mean, member, counts, first, outs):
    acc, sums = part_gram
    columns = panel.shape[1]
    width = acc.shape[0]
    tile = min(256, width)
    chunk = min(1024, columns)
    slots = min(8, width // tile * (columns // chunk))
    inputs = [*parts, *last, acc, sums, panel, mean, member, counts]
    specs = [WHOLE] * len(inputs)
    aliases = {}
    if first:
        aliases = {len(inputs): 0, len(inputs) + 1: 1}
        inputs += outs
        specs += [ANY] * 2
    cov, cross = outs
    return pl.pallas_call(
        functools.partial(late_kernel, (len(parts), len(last)), first, tile),
        out_shape=[jax.ShapeDtypeStruct(cov.shape, cov.dtype), jax.ShapeDtypeStruct(cross.shape, cross.dtype)],
        in_specs=specs,
        out_specs=[ANY, ANY],
        scratch_shapes=[
            pltpu.VMEM((width, last[0].shape[0]), jnp.bfloat16),
            pltpu.VMEM((slots, tile, chunk), jnp.float32),
            pltpu.VMEM(cross.shape, jnp.float32),
            pltpu.SemaphoreType.DMA((slots,)),
            pltpu.SemaphoreType.DMA,
        ],
        input_output_aliases=aliases,
        compiler_params=params(14),
        cost_estimate=pl.CostEstimate(flops=0, bytes_accessed=2 * MIB, transcendentals=0),
    )(*inputs)


def kernel(body, shapes, inputs, specs=None, mib=8, scratch=(), cost=COST):
    return pl.pallas_call(
        body,
        out_shape=[jax.ShapeDtypeStruct(shape, dtype) for shape, dtype in shapes],
        in_specs=specs or [WHOLE] * len(inputs),
        out_specs=[WHOLE] * len(shapes),
        scratch_shapes=scratch,
        compiler_params=params(mib),
        cost_estimate=cost,
    )(*inputs)


def gather_line(rows, shard, widths):
    with jax.named_scope("planes_far"):
        far = swap_cols(rows, 2)
    with jax.named_scope("planes_near"):
        near = swap_cols(rows, 1)
    with jax.named_scope("chips"):
        half = shard.shape[0] // 2
        sides = [swap_rows(shard, 2), swap_rows(shard, 4)]
        corner = [swap_rows(sides[1][:half], 2), swap_rows(sides[0][half:], 4)]
        shards = [shard, *sides, *corner]
    shards, rows, near, far = lax.optimization_barrier((shards, rows, near, far))
    cuts = kernel(functools.partial(cut_kernel, 2), [((rows.shape[0], width), rows.dtype) for width in widths] * 2, [rows, far])
    (stacked,) = kernel(stack_kernel, [((4 * shard.shape[0], *shard.shape[1:]), shard.dtype)], shards)
    with jax.named_scope("cores"):
        other = swap_rows(stacked, 1)
    groups = []
    for index in range(len(widths)):
        own, passed = cuts[index :: len(widths)]
        with jax.named_scope("planes_last"):
            last = (swap_cols(passed, 1), pair_cols(own, 1))
        groups.append([(rows,), (near,), (far,), last])
    return groups, stacked, other


def gather(rows, shard, widths):
    chips = lax.axis_size("row") // 2
    planes = lax.axis_size("col")
    if chips == 4 and planes == 4:
        return gather_line(rows, shard, widths)
    arrays = [(rows,)] + [(swap_cols(rows, mask),) for mask in range(1, planes)]
    starts = [sum(widths[:index]) for index in range(len(widths))]
    last = [arrays[-1][0][:, start : start + width] for start, width in zip(starts, widths)]
    shards = [shard] + [swap_rows(shard, 2 * mask) for mask in range(1, chips)]
    (stacked,) = kernel(stack_kernel, [((chips * shard.shape[0], *shard.shape[1:]), shard.dtype)], shards, mib=40)
    return [[*arrays[:-1], (part,)] for part in last], stacked, swap_rows(stacked, 1)


def shards(activations, tenant_ids, concept_labels):
    local, width = activations.shape
    rows = lax.axis_size("row")
    planes = lax.axis_size("col")
    chips = rows // 2
    block = width // rows
    panel_width = width // planes
    total = local * rows * planes
    groups = TENANTS * LABELS
    half = jnp.bfloat16

    dealt = kernel(
        functools.partial(deal_kernel, chips),
        [((local, 2 * block), half)] * chips + [((local, panel_width + LANES), half)] * planes,
        [tenant_ids * LABELS + concept_labels, activations],
        [ANY, ANY],
        scratch=[
            pltpu.VMEM((local, width), half),
            pltpu.SMEM((local,), jnp.int32),
            pltpu.SemaphoreType.DMA((2,)),
        ],
    )
    to_rows, to_cols = dealt[:chips], dealt[chips:]
    col_parts = [to_cols[0]] + [swap_cols(to_cols[mask], mask) for mask in range(1, planes)]
    row_parts = [to_rows[0]] + [swap_rows(to_rows[mask], 2 * mask) for mask in range(1, chips)]
    row_parts, col_parts[2] = lax.optimization_barrier((row_parts, col_parts[2]))
    half_shape = (chips, local, block // 2)
    shared = kernel(functools.partial(share_kernel, chips), [(half_shape, half)] * 2, row_parts)
    shared = [swap_rows(part, 1) for part in shared]
    shared, col_parts = lax.optimization_barrier((shared, col_parts))
    (row_shard,) = kernel(functools.partial(rows_kernel, chips), [((rows * local, block), half)], [*row_parts, *shared])
    slice_width = block // planes
    cut = slice_width * (planes // 2)
    widths = (cut, block - cut)
    shard_shape = (planes, local, panel_width + LANES)
    col_parts = [part.reshape(1, *part.shape) for part in col_parts]
    (col_shard,) = kernel(stack_kernel, [(shard_shape, half)], col_parts)

    pieces, near, far = gather(row_shard, col_shard, widths)
    panel, mean, member, counts = kernel(
        functools.partial(column_kernel, chips),
        [((total, panel_width), half), ((8, panel_width), jnp.float32), ((total, groups), half), ((groups, LANES), jnp.float32)],
        [near, far],
        mib=10,
    )

    outs = (
        jax.ShapeDtypeStruct((block, panel_width), jnp.float32),
        jax.ShapeDtypeStruct((groups, slice_width), jnp.float32),
    )
    (*parts, last), *others = pieces
    parts = [part for (part,) in parts]
    part_gram = early(parts, panel, 0, widths[0])
    outs = late(parts, last, part_gram, panel, mean, member, counts, 0, outs)
    first = widths[0]
    for piece, size in zip(others, widths[1:]):
        outs = gram(piece, panel, mean, member, counts, first, size, outs)
        first += size
    return tuple(outs)


def solution(mesh):
    placed = (P(("row", "col"), None), P(("row", "col")), P(("row", "col")))
    return jax.shard_map(
        shards,
        mesh=mesh,
        in_specs=placed,
        out_specs=(P("row", "col"), P(None, ("row", "col"))),
        check_vma=False,
    )
```

```python
import functools

import jax
import jax.numpy as jnp
from jax import lax
from jax.experimental import pallas as pl
from jax.experimental.pallas import tpu as pltpu
from jax.sharding import PartitionSpec as P

TENANTS = 64
LABELS = 2
LANES = 128
MIB = 1024 * 1024

COST = pl.CostEstimate(flops=0, bytes_accessed=0, transcendentals=0)

ANY = pl.BlockSpec(memory_space=pl.ANY)
WHOLE = pl.BlockSpec(memory_space=pltpu.VMEM)


def params(mib):
    return pltpu.CompilerParams(vmem_limit_bytes=mib * MIB)


def swap_rows(x, mask):
    return lax.ppermute(x, "row", [(i, i ^ mask) for i in range(lax.axis_size("row"))])


def swap_cols(x, mask):
    return lax.ppermute(x, "col", [(i, i ^ mask) for i in range(lax.axis_size("col"))])


def pair_cols(x, first):
    count = lax.axis_size("col")
    partner = {i: i for i in range(count)}
    for low in range(first, count - 1, 2):
        partner[low], partner[low + 1] = low + 1, low
    return lax.ppermute(x, "col", list(partner.items()))


def place():
    row = lax.axis_index("row")
    return row // 2, row % 2, lax.axis_index("col")


def deal_kernel(chips, codes_hbm, features_hbm, *refs):
    *outs, features, groups, sems = refs
    loads = [
        pltpu.make_async_copy(features_hbm, features, sems.at[0]),
        pltpu.make_async_copy(codes_hbm, groups, sems.at[1]),
    ]
    for load in loads:
        load.start()
    for load in loads:
        load.wait()
    local, total = features.shape
    chip, _, col = place()
    row_outs, col_outs = outs[:chips], outs[chips:]
    width = total // len(col_outs)
    token = lax.broadcasted_iota(jnp.int32, (local, LANES), 0)
    codes = jnp.zeros((local, LANES), jnp.int32)
    for index in range(local):
        codes = jnp.where(token == index, groups[index], codes)
    codes = codes.astype(jnp.float32).astype(jnp.bfloat16)
    for mask, out in enumerate(col_outs):
        start = pl.multiple_of((col ^ mask) * width, LANES)
        out[:, :width] = features[:, pl.ds(start, width)]
        out[:, width:] = codes
    for mask, out in enumerate(row_outs):
        block = out.shape[1]
        start = pl.multiple_of((chip ^ mask) * block, LANES)
        out[...] = features[:, pl.ds(start, block)]


def share_kernel(parts, *refs):
    _, core, _ = place()
    outs = refs[parts:]
    width = outs[0].shape[2]
    for side, out in enumerate(outs):
        start = pl.multiple_of(((1 - core) * len(outs) + side) * width, LANES)
        for index, part in enumerate(refs[:parts]):
            out[index] = part[:, pl.ds(start, width)]


def rows_kernel(parts, *refs):
    *shared, out = refs[parts:]
    _, core, _ = place()
    local, width = shared[0].shape[1:]
    begin = pl.multiple_of(core * out.shape[1], LANES)
    for index, part in enumerate(refs[:parts]):
        rows = pl.ds(index * 2 * local, 2 * local)
        for side, other in enumerate(shared):
            own = part[:, pl.ds(begin + side * width, width)]
            out[rows, side * width : (side + 1) * width] = jnp.concatenate([own, other[index]], axis=0)


def cut_kernel(arrays, *refs):
    outs = refs[arrays:]
    for index, array in enumerate(refs[:arrays]):
        start = 0
        for out in outs[index * len(outs) // arrays : (index + 1) * len(outs) // arrays]:
            out[...] = array[:, start : start + out.shape[1]]
            start += out.shape[1]


def stack_kernel(*refs):
    *parts, out = refs
    start = 0
    for part in parts:
        rows = part.shape[0]
        out[start : start + rows] = part[...]
        start += rows


def column_kernel(chips, *refs):
    near, far, panel, mean, member, counts = refs
    total, columns = panel.shape
    _, local, _ = near.shape
    planes = near.shape[0] // chips
    step = min(512, columns)
    ones = jnp.ones((16, total), jnp.bfloat16)
    lanes = lax.broadcasted_iota(jnp.int32, (2 * local, LANES), 1).astype(jnp.float32)
    for start in range(0, columns, step):
        span = pl.ds(start, step)
        for plane in range(planes):
            for chip in range(chips):
                both = jnp.concatenate([near[chip * planes + plane, :, span], far[chip * planes + plane, :, span]], axis=0)
                target = (plane * chips + chip) * 2 * local
                panel[target : target + 2 * local, span] = both
                if start == 0:
                    code = pl.ds(columns, LANES)
                    both = jnp.concatenate([near[chip * planes + plane, :, code], far[chip * planes + plane, :, code]], axis=0)
                    member[target : target + 2 * local, :] = (both.astype(jnp.float32) == lanes).astype(jnp.bfloat16)
        sums = jnp.dot(ones, panel[:, span], preferred_element_type=jnp.float32)
        mean[:, span] = sums[:8] / total
    ones = jnp.ones((total, LANES), jnp.bfloat16)
    counts[...] = lax.dot_general(member[...], ones, (((0,), (0,)), ((), ())), preferred_element_type=jnp.float32)


def gram_kernel(pairs, first, tile, *refs):
    parts, refs = refs[: sum(pairs)], refs[sum(pairs) :]
    panel, mean, member, counts = refs[:4]
    cov, cross, left_ref, out_ref, cross_ref, out_sem, cross_sem = refs[-7:]
    _, _, col = place()
    total, columns = panel.shape
    width = left_ref.shape[0]
    slice_width = cross_ref.shape[1]
    chunk = out_ref.shape[2]
    inside = (col > 0) & (col < len(pairs) - 1)

    def features(start, size):
        blocks, index = [], 0
        for count in pairs:
            both = []
            for part in parts[index : index + count]:
                offset = first if part.shape[1] > width else 0
                both.append(part[:, pl.ds(start + offset, size)])
            blocks.append(both[0] if count == 1 else jnp.where(inside, both[1], both[0]))
            index += count
        return jnp.concatenate(blocks, axis=0)

    slots = out_ref.shape[0]
    per_row = columns // chunk
    steps = width // tile * per_row

    def store(step):
        slot = step % slots
        target = cov.at[pl.ds(first + step // per_row * tile, tile), pl.ds(step % per_row * chunk, chunk)]
        return pltpu.make_async_copy(out_ref.at[slot], target, out_sem.at[slot])

    ones = jnp.ones((total, LANES), jnp.bfloat16)
    for step in range(steps):
        if step >= slots:
            store(step - slots).wait()
        rows = pl.ds(step // per_row * tile, tile)
        if step % per_row == 0:
            left = features(step // per_row * tile, tile).T
            left_ref[rows, :] = left
            row_mean = jnp.dot(left, ones, preferred_element_type=jnp.float32)[:, :1] / total
        span = pl.ds(step % per_row * chunk, chunk)
        gram = jnp.dot(left_ref[rows, :], panel[:, span], preferred_element_type=jnp.float32)
        out_ref[step % slots] = gram * (1.0 / total) - row_mean * mean[:1, span]
        store(step).start()

    begin = col * slice_width - first
    mine = (begin >= 0) & (begin < width)
    save = pltpu.make_async_copy(cross_ref, cross, cross_sem)

    @pl.when(mine)
    def _():
        own = features(pl.multiple_of(begin, LANES), slice_width)
        sums = lax.dot_general(member[...], own, (((0,), (0,)), ((), ())), preferred_element_type=jnp.float32)
        slice_mean = jnp.dot(jnp.ones((16, total), jnp.bfloat16), own, preferred_element_type=jnp.float32)[:1] / total
        groups = member.shape[1]
        cross_ref[...] = (groups / total) * (sums - counts[:, :1] * slice_mean)
        save.start()

    for step in range(max(0, steps - slots), steps):
        store(step).wait()
    pl.when(mine)(save.wait)


def gram(groups, panel, mean, member, counts, first, width, outs):
    total, columns = panel.shape
    tile = min(256, width)
    chunk = min(1024, columns)
    slots = min(16, width // tile * (columns // chunk))
    parts = [part for group in groups for part in group]
    inputs = [*parts, panel, mean, member, counts]
    specs = [WHOLE] * len(inputs)
    aliases = {}
    if first:
        aliases = {len(inputs): 0, len(inputs) + 1: 1}
        inputs += outs
        specs += [ANY] * 2
    cov, cross = outs
    return pl.pallas_call(
        functools.partial(gram_kernel, tuple(map(len, groups)), first, tile),
        out_shape=[jax.ShapeDtypeStruct(cov.shape, cov.dtype), jax.ShapeDtypeStruct(cross.shape, cross.dtype)],
        in_specs=specs,
        out_specs=[ANY, ANY],
        scratch_shapes=[
            pltpu.VMEM((width, total), jnp.bfloat16),
            pltpu.VMEM((slots, tile, chunk), jnp.float32),
            pltpu.VMEM(cross.shape, jnp.float32),
            pltpu.SemaphoreType.DMA((slots,)),
            pltpu.SemaphoreType.DMA,
        ],
        input_output_aliases=aliases,
        compiler_params=params(25),
        cost_estimate=pl.CostEstimate(flops=0, bytes_accessed=2 * MIB, transcendentals=0),
    )(*inputs)


def early_kernel(first, tile, *refs):
    *parts, panel, acc, sums, left_ref = refs
    width, depth = left_ref.shape
    columns = panel.shape[1]
    chunk = min(2048, columns)
    ones = jnp.ones((depth, LANES), jnp.bfloat16)
    for start in range(0, width, tile):
        rows = pl.ds(start, tile)
        left = jnp.concatenate([part[:, pl.ds(first + start, tile)] for part in parts], axis=0).T
        left_ref[rows, :] = left
        sums[rows, :] = jnp.dot(left, ones, preferred_element_type=jnp.float32)
    for start in range(0, width, tile):
        rows = pl.ds(start, tile)
        for begin in range(0, columns, chunk):
            span = pl.ds(begin, chunk)
            acc[rows, span] = jnp.dot(left_ref[rows, :], panel[:depth, span], preferred_element_type=jnp.float32)


def early(parts, panel, first, width):
    shard = parts[0].shape[0]
    depth = shard * len(parts)
    return kernel(
        functools.partial(early_kernel, first, min(256, width)),
        [((width, panel.shape[1]), jnp.float32), ((width, LANES), jnp.float32)],
        [*parts, panel],
        mib=10,
        scratch=[pltpu.VMEM((width, depth), jnp.bfloat16)],
    )


def late_kernel(count, first, tile, *refs):
    parts, last, refs = refs[: count[0]], refs[count[0] : sum(count)], refs[sum(count) :]
    acc, sums, panel, mean, member, counts = refs[:6]
    cov, cross, left_ref, out_ref, cross_ref, out_sem, cross_sem = refs[-7:]
    _, _, col = place()
    total, columns = panel.shape
    width, depth = left_ref.shape
    slice_width = cross_ref.shape[1]
    chunk = out_ref.shape[2]
    inside = (col > 0) & (col < count[0])

    def latest(start, size):
        both = [part[:, pl.ds(start, size)] for part in last]
        return both[0] if len(both) == 1 else jnp.where(inside, both[1], both[0])

    slots = out_ref.shape[0]
    per_row = columns // chunk
    steps = width // tile * per_row

    def store(step):
        slot = step % slots
        target = cov.at[pl.ds(first + step // per_row * tile, tile), pl.ds(step % per_row * chunk, chunk)]
        return pltpu.make_async_copy(out_ref.at[slot], target, out_sem.at[slot])

    ones = jnp.ones((depth, LANES), jnp.bfloat16)
    for step in range(steps):
        if step >= slots:
            store(step - slots).wait()
        rows = pl.ds(step // per_row * tile, tile)
        if step % per_row == 0:
            left = latest(step // per_row * tile, tile).T
            left_ref[rows, :] = left
            row_sum = sums[rows, :] + jnp.dot(left, ones, preferred_element_type=jnp.float32)
            row_mean = row_sum[:, :1] / total
        span = pl.ds(step % per_row * chunk, chunk)
        gram = acc[rows, span] + jnp.dot(left_ref[rows, :], panel[total - depth :, span], preferred_element_type=jnp.float32)
        out_ref[step % slots] = gram * (1.0 / total) - row_mean * mean[:1, span]
        store(step).start()

    begin = col * slice_width - first
    mine = (begin >= 0) & (begin < width)
    save = pltpu.make_async_copy(cross_ref, cross, cross_sem)

    @pl.when(mine)
    def _():
        place_in_row = pl.multiple_of(col * slice_width, LANES)
        blocks = [part[:, pl.ds(place_in_row, slice_width)] for part in parts]
        own = jnp.concatenate([*blocks, latest(pl.multiple_of(begin, LANES), slice_width)], axis=0)
        group_sums = lax.dot_general(member[...], own, (((0,), (0,)), ((), ())), preferred_element_type=jnp.float32)
        slice_mean = jnp.dot(jnp.ones((16, total), jnp.bfloat16), own, preferred_element_type=jnp.float32)[:1] / total
        groups = member.shape[1]
        cross_ref[...] = (groups / total) * (group_sums - counts[:, :1] * slice_mean)
        save.start()

    for step in range(max(0, steps - slots), steps):
        store(step).wait()
    pl.when(mine)(save.wait)


def late(parts, last, part_gram, panel, mean, member, counts, first, outs):
    acc, sums = part_gram
    columns = panel.shape[1]
    width = acc.shape[0]
    tile = min(256, width)
    chunk = min(1024, columns)
    slots = min(12, width // tile * (columns // chunk))
    inputs = [*parts, *last, acc, sums, panel, mean, member, counts]
    specs = [WHOLE] * len(inputs)
    aliases = {}
    if first:
        aliases = {len(inputs): 0, len(inputs) + 1: 1}
        inputs += outs
        specs += [ANY] * 2
    cov, cross = outs
    return pl.pallas_call(
        functools.partial(late_kernel, (len(parts), len(last)), first, tile),
        out_shape=[jax.ShapeDtypeStruct(cov.shape, cov.dtype), jax.ShapeDtypeStruct(cross.shape, cross.dtype)],
        in_specs=specs,
        out_specs=[ANY, ANY],
        scratch_shapes=[
            pltpu.VMEM((width, last[0].shape[0]), jnp.bfloat16),
            pltpu.VMEM((slots, tile, chunk), jnp.float32),
            pltpu.VMEM(cross.shape, jnp.float32),
            pltpu.SemaphoreType.DMA((slots,)),
            pltpu.SemaphoreType.DMA,
        ],
        input_output_aliases=aliases,
        compiler_params=params(18),
        cost_estimate=pl.CostEstimate(flops=0, bytes_accessed=2 * MIB, transcendentals=0),
    )(*inputs)


def kernel(body, shapes, inputs, specs=None, mib=8, scratch=(), cost=COST):
    return pl.pallas_call(
        body,
        out_shape=[jax.ShapeDtypeStruct(shape, dtype) for shape, dtype in shapes],
        in_specs=specs or [WHOLE] * len(inputs),
        out_specs=[WHOLE] * len(shapes),
        scratch_shapes=scratch,
        compiler_params=params(mib),
        cost_estimate=cost,
    )(*inputs)


def gather_line(rows, shard, widths):
    with jax.named_scope("planes_far"):
        far = swap_cols(rows, 2)
    with jax.named_scope("planes_near"):
        near = swap_cols(rows, 1)
    with jax.named_scope("chips"):
        half = shard.shape[0] // 2
        sides = [swap_rows(shard, 2), swap_rows(shard, 4)]
        corner = [swap_rows(sides[1][:half], 2), swap_rows(sides[0][half:], 4)]
        shards = [shard, *sides, *corner]
    shards, rows, near, far = lax.optimization_barrier((shards, rows, near, far))
    cuts = kernel(functools.partial(cut_kernel, 2), [((rows.shape[0], width), rows.dtype) for width in widths] * 2, [rows, far])
    (stacked,) = kernel(stack_kernel, [((4 * shard.shape[0], *shard.shape[1:]), shard.dtype)], shards)
    with jax.named_scope("cores"):
        other = swap_rows(stacked, 1)
    groups = []
    for index in range(len(widths)):
        own, passed = cuts[index :: len(widths)]
        with jax.named_scope("planes_last"):
            last = (swap_cols(passed, 1), pair_cols(own, 1))
        groups.append([(rows,), (near,), (far,), last])
    return groups, stacked, other


def gather(rows, shard, widths):
    chips = lax.axis_size("row") // 2
    planes = lax.axis_size("col")
    if chips == 4 and planes == 4:
        return gather_line(rows, shard, widths)
    arrays = [(rows,)] + [(swap_cols(rows, mask),) for mask in range(1, planes)]
    starts = [sum(widths[:index]) for index in range(len(widths))]
    last = [arrays[-1][0][:, start : start + width] for start, width in zip(starts, widths)]
    shards = [shard] + [swap_rows(shard, 2 * mask) for mask in range(1, chips)]
    (stacked,) = kernel(stack_kernel, [((chips * shard.shape[0], *shard.shape[1:]), shard.dtype)], shards, mib=40)
    return [[*arrays[:-1], (part,)] for part in last], stacked, swap_rows(stacked, 1)


def shards(activations, tenant_ids, concept_labels):
    local, width = activations.shape
    rows = lax.axis_size("row")
    planes = lax.axis_size("col")
    chips = rows // 2
    block = width // rows
    panel_width = width // planes
    total = local * rows * planes
    groups = TENANTS * LABELS
    half = jnp.bfloat16

    dealt = kernel(
        functools.partial(deal_kernel, chips),
        [((local, 2 * block), half)] * chips + [((local, panel_width + LANES), half)] * planes,
        [tenant_ids * LABELS + concept_labels, activations],
        [ANY, ANY],
        scratch=[
            pltpu.VMEM((local, width), half),
            pltpu.SMEM((local,), jnp.int32),
            pltpu.SemaphoreType.DMA((2,)),
        ],
    )
    to_rows, to_cols = dealt[:chips], dealt[chips:]
    col_parts = [to_cols[0]] + [swap_cols(to_cols[mask], mask) for mask in range(1, planes)]
    row_parts = [to_rows[0]] + [swap_rows(to_rows[mask], 2 * mask) for mask in range(1, chips)]
    row_parts, col_parts[2] = lax.optimization_barrier((row_parts, col_parts[2]))
    half_shape = (chips, local, block // 2)
    shared = kernel(functools.partial(share_kernel, chips), [(half_shape, half)] * 2, row_parts)
    shared = [swap_rows(part, 1) for part in shared]
    shared, col_parts = lax.optimization_barrier((shared, col_parts))
    (row_shard,) = kernel(functools.partial(rows_kernel, chips), [((rows * local, block), half)], [*row_parts, *shared])
    slice_width = block // planes
    cut = slice_width * (planes // 2)
    widths = (cut, block - cut)
    shard_shape = (planes, local, panel_width + LANES)
    col_parts = [part.reshape(1, *part.shape) for part in col_parts]
    (col_shard,) = kernel(stack_kernel, [(shard_shape, half)], col_parts)

    pieces, near, far = gather(row_shard, col_shard, widths)
    panel, mean, member, counts = kernel(
        functools.partial(column_kernel, chips),
        [((total, panel_width), half), ((8, panel_width), jnp.float32), ((total, groups), half), ((groups, LANES), jnp.float32)],
        [near, far],
        mib=10,
    )

    outs = (
        jax.ShapeDtypeStruct((block, panel_width), jnp.float32),
        jax.ShapeDtypeStruct((groups, slice_width), jnp.float32),
    )
    (*parts, last), *others = pieces
    parts = [part for (part,) in parts]
    part_gram = early(parts, panel, 0, widths[0])
    outs = late(parts, last, part_gram, panel, mean, member, counts, 0, outs)
    first = widths[0]
    for piece, size in zip(others, widths[1:]):
        outs = gram(piece, panel, mean, member, counts, first, size, outs)
        first += size
    return tuple(outs)


def solution(mesh):
    placed = (P(("row", "col"), None), P(("row", "col")), P(("row", "col")))
    return jax.shard_map(
        shards,
        mesh=mesh,
        in_specs=placed,
        out_specs=(P("row", "col"), P(None, ("row", "col"))),
        check_vma=False,
    )
```
